32 devices in a mesh: occ: 16 (over z, y, x), aux: 2 (over core).
Axes of the slice: x: 2, y: 2, z: 4, core: 2. Of those that a mesh axis runs over, the one named last changes fastest.
Arguments:
- b_rows: bfloat16 [12288, 2048], P('aux', 'occ'), may hold values from -0.5 to 0.5
- b_cols: bfloat16 [12288, 8192], P('aux', 'occ'), may hold values from -0.5 to 0.5
- eps_occ: float32 [32], replicated, may hold values from -1.5 to -0.3
- eps_va: float32 [64], replicated, may hold values from 0.2 to 2
- eps_vb: float32 [256], replicated, may hold values from 0.2 to 2
Outputs:
- gamma: float32 [12288, 2048], P('aux', 'occ')
The draws below stay inside these ranges and needn't reach their ends.
All inputs are finite; a program needn't handle non-finite values.
Results may differ from the reference program's by a relative error of at most 0.0027.
Values may be sent and summed in bfloat16 or wider, within the bound.
A program may use at most 64 MiB of HBM per device.

```python
import jax
import jax.numpy as jnp
from jax import lax

NAUX = 12288
VA = 64
VB = 256
OCC_DEV = 2
NOCC = 32
N_OCC = 16


def levels(own_key, dims, shards, least, high):
    def one(axis_at, parts):
        steps = jax.random.uniform(jax.random.fold_in(jax.random.fold_in(own_key, 6), axis_at), (parts,), jnp.float32, least / len(shards), high / len(shards))
        return jnp.repeat(jnp.exp(steps), dims[axis_at] // parts).reshape((-1,) + (1,) * (len(dims) - axis_at - 1))

    factor_of = one(*shards[0])
    for cut in shards[1:]:
        factor_of = factor_of * one(*cut)
    return factor_of


def centred(stream_key, dims, spread, bound, split=(), kind=jnp.bfloat16):
    entries = jax.random.normal(stream_key, dims, jnp.float32) * spread
    if len(split) > 0:
        entries = levels(stream_key, dims, split, -0.22, 0.18) * entries
    return jnp.clip(entries, min=-bound, max=bound).astype(kind)


def setup_inputs(seed: int = 0) -> dict:
    key_list = jax.random.split(jax.random.key(seed), 6)
    return {
        "b_rows": centred(key_list[0], (NAUX, NOCC * VA), 0.08, 0.5, ((0, 2), (1, 16))),
        "b_cols": centred(key_list[1], (NAUX, NOCC * VB), 0.08, 0.5, ((0, 2), (1, 16))),
        "eps_occ": jnp.clip(jax.random.uniform(key_list[2], (NOCC,), jnp.float32, -1.5, -0.3), -1.5, -0.3),
        "eps_va": jnp.clip(jax.random.uniform(key_list[3], (VA,), jnp.float32, 0.2, 2.0), 0.2, 2.0),
        "eps_vb": jnp.clip(jax.random.uniform(key_list[4], (VB,), jnp.float32, 0.2, 2.0), 0.2, 2.0),
    }


spin_scale = 1.3


def energy_row(eps_occ, virt_energy, which, per_block):
    occ_energy = lax.dynamic_slice_in_dim(eps_occ, which * per_block, per_block)
    return (virt_energy[None, :] - occ_energy[:, None]).reshape(-1)


def reference(b_rows, b_cols, eps_occ, eps_va, eps_vb):
    width_rows = OCC_DEV * VA
    width_cols = OCC_DEV * VB

    def one_block(which):
        left_block = lax.dynamic_slice_in_dim(b_rows, which * width_rows, width_rows, 1)
        row_energy = energy_row(eps_occ, eps_va, which, OCC_DEV)
        total = jnp.zeros((NAUX, width_rows), jnp.float32)
        for shift_index in range(3):
            partner = ((which - shift_index) % N_OCC).astype(jnp.int32)
            right_block = lax.dynamic_slice_in_dim(b_cols, partner * width_cols, width_cols, 1)
            col_energy = energy_row(eps_occ, eps_vb, partner, OCC_DEV)
            summed = lax.dot_general(left_block, right_block, (((0,), (0,)), ((), ())), preferred_element_type=jnp.float32)
            amplitude = (spin_scale * summed / (row_energy[:, None] + col_energy[None, :])).astype(jnp.bfloat16)
            total = total + lax.dot_general(right_block, amplitude, (((1,), (1,)), ((), ())), preferred_element_type=jnp.float32)
        return total

    blocks = lax.map(one_block, jnp.arange(N_OCC, dtype=jnp.int32))
    return jnp.transpose(blocks, (1, 0, 2)).reshape(NAUX, N_OCC * width_rows)
```

```python
import functools

import jax
import jax.numpy as jnp
from jax import lax
from jax.experimental import pallas as pl
from jax.experimental.pallas import tpu as pltpu
from jax.sharding import PartitionSpec as P

spin_scale = 1.3
MESH = pl.DeviceIdType.MESH
CHUNKS = 16


def kernel(
    n, n_aux, chunks,
    rows_hbm, cols_hbm, occ_ref, va_ref, vb_ref, out_hbm,
    cols, own, rows1, rows2, v, v_in, factor, amp, g1_out, g2_out, g1_in, g2_in, g2, total,
    cols_sem, own_sem, out_sem, rows_send, rows_recv, g_send, g_recv, v_send, v_recv,
):
    p = lax.axis_index("occ")
    a = lax.axis_index("aux")
    depth, width = rows_hbm.shape
    wide = cols_hbm.shape[1]
    ch = depth // chunks
    two_down = lax.rem(p + (n - 2), n)
    two_up = lax.rem(p + 2, n)
    odd = lax.rem(p, 2)
    pair = p + 1 - 2 * odd

    def part(c):
        return pl.ds(pl.multiple_of(c * ch, ch), ch)

    def rows_two(c):
        return pltpu.make_async_remote_copy(
            src_ref=rows_hbm.at[part(c)], dst_ref=rows2.at[part(c)],
            send_sem=rows_send.at[1, c], recv_sem=rows_recv.at[1, c],
            device_id=(two_down, a), device_id_type=MESH)

    def rows_one_odd(c):
        return pltpu.make_async_remote_copy(
            src_ref=rows_hbm.at[part(c)], dst_ref=rows1.at[part(c)],
            send_sem=rows_send.at[0, c], recv_sem=rows_recv.at[0, c],
            device_id=(pair, a), device_id_type=MESH)

    def rows_one_even(c):
        return pltpu.make_async_remote_copy(
            src_ref=rows2.at[part(c)], dst_ref=rows1.at[part(c)],
            send_sem=rows_send.at[0, c], recv_sem=rows_recv.at[0, c],
            device_id=(pair, a), device_id_type=MESH)

    def gamma_one(c):
        return pltpu.make_async_remote_copy(
            src_ref=g1_out.at[part(c)], dst_ref=g1_in.at[part(c)],
            send_sem=g_send.at[0, c], recv_sem=g_recv.at[0, c],
            device_id=(pair, a), device_id_type=MESH)

    def gamma_two(c):
        return pltpu.make_async_remote_copy(
            src_ref=g2_out.at[part(c)], dst_ref=g2_in.at[part(c)],
            send_sem=g_send.at[1, c], recv_sem=g_recv.at[1, c],
            device_id=(two_up, a), device_id_type=MESH)

    def v_copy(s, d):
        return pltpu.make_async_remote_copy(
            src_ref=v.at[s], dst_ref=v_in.at[d - 1, s],
            send_sem=v_send.at[d - 1, s], recv_sem=v_recv.at[d - 1, s],
            device_id=(p, lax.rem(a + d, n_aux)), device_id_type=MESH)

    def cols_copy(c):
        return pltpu.make_async_copy(cols_hbm.at[part(c)], cols.at[part(c)], cols_sem.at[c])

    def own_copy(c):
        return pltpu.make_async_copy(rows_hbm.at[part(c)], own.at[part(c)], own_sem.at[c])

    def out_copy(c):
        return pltpu.make_async_copy(total.at[part(c)], out_hbm.at[part(c)], out_sem.at[c])

    barrier = pltpu.get_barrier_semaphore()
    peers = [(two_down, a), (two_up, a), (pair, a)]
    peers += [(p, lax.rem(a + d, n_aux)) for d in range(1, n_aux)]
    for peer in peers:
        pl.semaphore_signal(barrier, inc=1, device_id=peer, device_id_type=MESH)

    @pl.loop(0, chunks)
    def _(c):
        cols_copy(c).start()
        own_copy(c).start()

    pl.semaphore_wait(barrier, len(peers))

    @pl.loop(0, chunks)
    def _(c):
        rows_two(c).start()

        @pl.when(odd == 1)
        def _():
            rows_one_odd(c).start()

    per_block = width // va_ref.shape[1]
    col = jnp.concatenate([vb_ref[...] - occ_ref[p * per_block + i] for i in range(per_block)], axis=1)
    for s in range(3):
        which = lax.rem(p + s, n)
        row = jnp.concatenate([va_ref[...] - occ_ref[which * per_block + i] for i in range(per_block)], axis=1)
        row = jnp.broadcast_to(row, (width, width)).T
        for at in range(0, wide, width):
            factor[s, :, at:at + width] = spin_scale / (row + col[:, at:at + width])
    v[...] = jnp.zeros_like(v)

    def integrals(s, left, c):
        v[s] += lax.dot_general(
            left[part(c), :], cols[part(c), :], (((0,), (0,)), ((), ())),
            preferred_element_type=jnp.float32)

    @pl.loop(0, chunks)
    def _(c):
        cols_copy(c).wait()
        own_copy(c).wait()
        integrals(0, own, c)
        rows_two(c).wait_recv()

        @pl.when(odd == 0)
        def _():
            rows_one_even(c).start()

        integrals(2, rows2, c)
        rows_one_odd(c).wait_recv()
        integrals(1, rows1, c)

    for s in (1, 2, 0):
        for d in range(1, n_aux):
            v_copy(s, d).start()

    def amplitude(s):
        summed = v[s]
        for d in range(1, n_aux):
            v_copy(s, d).wait_recv()
            summed += v_in[d - 1, s]
        amp[s * width:(s + 1) * width, :] = (summed * factor[s]).astype(jnp.bfloat16)

    def pieces(c, first, last):
        return lax.dot_general(
            cols[part(c), :], amp[first * width:last * width, :], (((1,), (1,)), ((), ())),
            preferred_element_type=jnp.float32)

    amplitude(1)
    amplitude(2)

    @pl.loop(0, chunks)
    def _(c):
        both = pieces(c, 1, 3)
        g1_out[part(c), :] = both[:, :width].astype(jnp.bfloat16)
        gamma_one(c).start()

        @pl.when(odd == 1)
        def _():
            g2_out[part(c), :] = both[:, width:].astype(jnp.bfloat16)
            gamma_two(c).start()

        @pl.when(odd == 0)
        def _():
            g2[part(c), :] = both[:, width:]

    amplitude(0)

    @pl.loop(0, chunks)
    def _(c):
        @pl.when(odd == 0)
        def _():
            gamma_one(c).wait_recv()
            g2_out[part(c), :] = (g2[part(c), :] + g1_in[part(c), :].astype(jnp.float32)).astype(jnp.bfloat16)
            gamma_two(c).start()

        total[part(c), :] = pieces(c, 0, 1)

    @pl.loop(0, chunks)
    def _(c):
        @pl.when(odd == 1)
        def _():
            gamma_one(c).wait_recv()
            total[part(c), :] += g1_in[part(c), :].astype(jnp.float32)

        gamma_two(c).wait_recv()
        total[part(c), :] += g2_in[part(c), :].astype(jnp.float32)
        out_copy(c).start()

    for s in range(3):
        for d in range(1, n_aux):
            v_copy(s, d).wait_send()

    @pl.loop(0, chunks)
    def _(c):
        rows_two(c).wait_send()
        rows_one_odd(c).wait_send()
        gamma_one(c).wait_send()
        gamma_two(c).wait_send()
        out_copy(c).wait()


def per_device(n, n_aux, b_rows, b_cols, eps_occ, eps_va, eps_vb):
    depth, width = b_rows.shape
    wide = b_cols.shape[1]
    chunks = CHUNKS
    f32, bf16 = jnp.float32, jnp.bfloat16
    dma = pltpu.SemaphoreType.DMA
    return pl.pallas_call(
        functools.partial(kernel, n, n_aux, chunks),
        out_shape=jax.ShapeDtypeStruct((depth, width), f32),
        in_specs=[
            pl.BlockSpec(memory_space=pl.ANY),
            pl.BlockSpec(memory_space=pl.ANY),
            pl.BlockSpec(memory_space=pltpu.SMEM),
            pl.BlockSpec(memory_space=pltpu.VMEM),
            pl.BlockSpec(memory_space=pltpu.VMEM),
        ],
        out_specs=pl.BlockSpec(memory_space=pl.ANY),
        scratch_shapes=[
            pltpu.VMEM((depth, wide), bf16),
            pltpu.VMEM((depth, width), bf16),
            pltpu.VMEM((depth, width), bf16),
            pltpu.VMEM((depth, width), bf16),
            pltpu.VMEM((3, width, wide), f32),
            pltpu.VMEM((n_aux - 1, 3, width, wide), f32),
            pltpu.VMEM((3, width, wide), f32),
            pltpu.VMEM((3 * width, wide), bf16),
            pltpu.VMEM((depth, width), bf16),
            pltpu.VMEM((depth, width), bf16),
            pltpu.VMEM((depth, width), bf16),
            pltpu.VMEM((depth, width), bf16),
            pltpu.VMEM((depth, width), f32),
            pltpu.VMEM((depth, width), f32),
            dma((chunks,)),
            dma((chunks,)),
            dma((chunks,)),
            dma((2, chunks)),
            dma((2, chunks)),
            dma((2, chunks)),
            dma((2, chunks)),
            dma((n_aux - 1, 3)),
            dma((n_aux - 1, 3)),
        ],
        compiler_params=pltpu.CompilerParams(
            collective_id=0, has_side_effects=True, vmem_limit_bytes=48 * 1024 * 1024),
        cost_estimate=pl.CostEstimate(
            flops=12 * depth * width * wide, bytes_accessed=2 * depth * (wide + 3 * width), transcendentals=0),
    )(b_rows, b_cols, eps_occ, eps_va[None, :], eps_vb[None, :])


def solution(mesh):
    return jax.shard_map(
        functools.partial(per_device, mesh.shape["occ"], mesh.shape["aux"]),
        mesh=mesh,
        in_specs=(P("aux", "occ"), P("aux", "occ"), P(), P(), P()),
        out_specs=P("aux", "occ"),
        check_vma=False,
    )
```

```python
import functools

import jax
import jax.numpy as jnp
from jax import lax
from jax.experimental import pallas as pl
from jax.experimental.pallas import tpu as pltpu
from jax.sharding import PartitionSpec as P

spin_scale = 1.3
MESH = pl.DeviceIdType.MESH
CHUNKS = 16


def kernel(
    n, n_aux, chunks,
    rows_hbm, cols_hbm, occ_hbm, va_hbm, vb_hbm, total,
    cols, own, rows1, rows2, v, v_in, factor, amp, g1_out, g2_out, g1_in, g2_in, g2, occ_ref, va_ref, vb_ref,
    energy_sem, cols_sem, own_sem, rows_send, rows_recv, g_send, g_recv, v_send, v_recv,
):
    p = lax.axis_index("occ")
    a = lax.axis_index("aux")
    depth, width = rows_hbm.shape
    wide = cols_hbm.shape[1]
    ch = depth // chunks
    two_down = lax.rem(p + (n - 2), n)
    two_up = lax.rem(p + 2, n)
    odd = lax.rem(p, 2)
    pair = p + 1 - 2 * odd

    def part(c):
        return pl.ds(pl.multiple_of(c * ch, ch), ch)

    def rows_two(c):
        return pltpu.make_async_remote_copy(
            src_ref=rows_hbm.at[part(c)], dst_ref=rows2.at[part(c)],
            send_sem=rows_send.at[1, c], recv_sem=rows_recv.at[1, c],
            device_id=(two_down, a), device_id_type=MESH)

    def rows_one_odd(c):
        return pltpu.make_async_remote_copy(
            src_ref=rows_hbm.at[part(c)], dst_ref=rows1.at[part(c)],
            send_sem=rows_send.at[0, c], recv_sem=rows_recv.at[0, c],
            device_id=(pair, a), device_id_type=MESH)

    def rows_one_even(c):
        return pltpu.make_async_remote_copy(
            src_ref=rows2.at[part(c)], dst_ref=rows1.at[part(c)],
            send_sem=rows_send.at[0, c], recv_sem=rows_recv.at[0, c],
            device_id=(pair, a), device_id_type=MESH)

    def gamma_one(c):
        return pltpu.make_async_remote_copy(
            src_ref=g1_out.at[part(c)], dst_ref=g1_in.at[part(c)],
            send_sem=g_send.at[0, c], recv_sem=g_recv.at[0, c],
            device_id=(pair, a), device_id_type=MESH)

    def gamma_two(c):
        return pltpu.make_async_remote_copy(
            src_ref=g2_out.at[part(c)], dst_ref=g2_in.at[part(c)],
            send_sem=g_send.at[1, c], recv_sem=g_recv.at[1, c],
            device_id=(two_up, a), device_id_type=MESH)

    def v_copy(s, d):
        return pltpu.make_async_remote_copy(
            src_ref=v.at[s], dst_ref=v_in.at[d - 1, s],
            send_sem=v_send.at[d - 1, s], recv_sem=v_recv.at[d - 1, s],
            device_id=(p, lax.rem(a + d, n_aux)), device_id_type=MESH)

    def cols_copy(c):
        return pltpu.make_async_copy(cols_hbm.at[part(c)], cols.at[part(c)], cols_sem.at[c])

    def own_copy(c):
        return pltpu.make_async_copy(rows_hbm.at[part(c)], own.at[part(c)], own_sem.at[c])

    barrier = pltpu.get_barrier_semaphore()
    peers = [(two_down, a), (two_up, a), (pair, a)]
    peers += [(p, lax.rem(a + d, n_aux)) for d in range(1, n_aux)]
    for peer in peers:
        pl.semaphore_signal(barrier, inc=1, device_id=peer, device_id_type=MESH)

    energies = [
        pltpu.make_async_copy(src, dst, energy_sem.at[i])
        for i, (src, dst) in enumerate([(occ_hbm, occ_ref), (va_hbm, va_ref), (vb_hbm, vb_ref)])
    ]
    for energy in energies:
        energy.start()
    pl.semaphore_wait(barrier, len(peers))

    @pl.loop(0, chunks)
    def _(c):
        rows_two(c).start()

        @pl.when(odd == 1)
        def _():
            rows_one_odd(c).start()

    @pl.loop(0, chunks)
    def _(c):
        cols_copy(c).start()
        own_copy(c).start()

    for energy in energies:
        energy.wait()
    per_block = width // va_ref.shape[1]
    col = jnp.concatenate([vb_ref[...] - occ_ref[p * per_block + i] for i in range(per_block)], axis=1)
    for s in range(3):
        which = lax.rem(p + s, n)
        row = jnp.concatenate([va_ref[...] - occ_ref[which * per_block + i] for i in range(per_block)], axis=1)
        row = jnp.broadcast_to(row, (width, width)).T
        for at in range(0, wide, width):
            factor[s, :, at:at + width] = spin_scale / (row + col[:, at:at + width])
    v[...] = jnp.zeros_like(v)

    def integrals(s, left, c):
        v[s] += lax.dot_general(
            left[part(c), :], cols[part(c), :], (((0,), (0,)), ((), ())),
            preferred_element_type=jnp.float32)

    @pl.loop(0, chunks)
    def _(c):
        cols_copy(c).wait()
        own_copy(c).wait()
        integrals(0, own, c)
        rows_two(c).wait_recv()

        @pl.when(odd == 0)
        def _():
            rows_one_even(c).start()

        integrals(2, rows2, c)
        rows_one_odd(c).wait_recv()
        integrals(1, rows1, c)

    for s in (1, 2, 0):
        for d in range(1, n_aux):
            v_copy(s, d).start()

    def amplitude(s):
        summed = v[s]
        for d in range(1, n_aux):
            v_copy(s, d).wait_recv()
            summed += v_in[d - 1, s]
        amp[s * width:(s + 1) * width, :] = (summed * factor[s]).astype(jnp.bfloat16)

    def pieces(c, first, last):
        return lax.dot_general(
            cols[part(c), :], amp[first * width:last * width, :], (((1,), (1,)), ((), ())),
            preferred_element_type=jnp.float32)

    amplitude(1)
    amplitude(2)

    @pl.loop(0, chunks)
    def _(c):
        both = pieces(c, 1, 3)
        g1_out[part(c), :] = both[:, :width].astype(jnp.bfloat16)
        gamma_one(c).start()

        @pl.when(odd == 1)
        def _():
            g2_out[part(c), :] = both[:, width:].astype(jnp.bfloat16)
            gamma_two(c).start()

        @pl.when(odd == 0)
        def _():
            g2[part(c), :] = both[:, width:]

    amplitude(0)

    @pl.loop(0, chunks)
    def _(c):
        @pl.when(odd == 0)
        def _():
            gamma_one(c).wait_recv()
            g2_out[part(c), :] = (g2[part(c), :] + g1_in[part(c), :].astype(jnp.float32)).astype(jnp.bfloat16)
            gamma_two(c).start()

        total[part(c), :] = pieces(c, 0, 1)

    @pl.loop(0, chunks)
    def _(c):
        @pl.when(odd == 1)
        def _():
            gamma_one(c).wait_recv()
            total[part(c), :] += g1_in[part(c), :].astype(jnp.float32)

        gamma_two(c).wait_recv()
        total[part(c), :] += g2_in[part(c), :].astype(jnp.float32)

    for s in range(3):
        for d in range(1, n_aux):
            v_copy(s, d).wait_send()

    @pl.loop(0, chunks)
    def _(c):
        rows_two(c).wait_send()
        rows_one_odd(c).wait_send()
        gamma_one(c).wait_send()
        gamma_two(c).wait_send()


def per_device(n, n_aux, b_rows, b_cols, eps_occ, eps_va, eps_vb):
    depth, width = b_rows.shape
    wide = b_cols.shape[1]
    chunks = CHUNKS
    f32, bf16 = jnp.float32, jnp.bfloat16
    dma = pltpu.SemaphoreType.DMA
    return pl.pallas_call(
        functools.partial(kernel, n, n_aux, chunks),
        out_shape=jax.ShapeDtypeStruct((depth, width), f32),
        in_specs=[
            pl.BlockSpec(memory_space=pltpu.HBM),
            pl.BlockSpec(memory_space=pltpu.HBM),
            pl.BlockSpec(memory_space=pltpu.HBM),
            pl.BlockSpec(memory_space=pltpu.HBM),
            pl.BlockSpec(memory_space=pltpu.HBM),
        ],
        out_specs=pl.BlockSpec(memory_space=pltpu.VMEM),
        scratch_shapes=[
            pltpu.VMEM((depth, wide), bf16),
            pltpu.VMEM((depth, width), bf16),
            pltpu.VMEM((depth, width), bf16),
            pltpu.VMEM((depth, width), bf16),
            pltpu.VMEM((3, width, wide), f32),
            pltpu.VMEM((n_aux - 1, 3, width, wide), f32),
            pltpu.VMEM((3, width, wide), f32),
            pltpu.VMEM((3 * width, wide), bf16),
            pltpu.VMEM((depth, width), bf16),
            pltpu.VMEM((depth, width), bf16),
            pltpu.VMEM((depth, width), bf16),
            pltpu.VMEM((depth, width), bf16),
            pltpu.VMEM((depth, width), f32),
            pltpu.SMEM(eps_occ.shape, f32),
            pltpu.VMEM((1, eps_va.shape[0]), f32),
            pltpu.VMEM((1, eps_vb.shape[0]), f32),
            dma((3,)),
            dma((chunks,)),
            dma((chunks,)),
            dma((2, chunks)),
            dma((2, chunks)),
            dma((2, chunks)),
            dma((2, chunks)),
            dma((n_aux - 1, 3)),
            dma((n_aux - 1, 3)),
        ],
        compiler_params=pltpu.CompilerParams(
            collective_id=0, has_side_effects=True, vmem_limit_bytes=48 * 1024 * 1024),
        cost_estimate=pl.CostEstimate(
            flops=12 * depth * width * wide, bytes_accessed=2 * depth * (wide + 3 * width), transcendentals=0),
    )(b_rows, b_cols, eps_occ, eps_va[None, :], eps_vb[None, :])


def solution(mesh):
    return jax.shard_map(
        functools.partial(per_device, mesh.shape["occ"], mesh.shape["aux"]),
        mesh=mesh,
        in_specs=(P("aux", "occ"), P("aux", "occ"), P(), P(), P()),
        out_specs=P("aux", "occ"),
        check_vma=False,
    )
```
